32 devices in a mesh: grp: 2 (over x), mk: 8 (over z, y), tile: 2 (over core).
Axes of the slice: x: 2, y: 2, z: 4, core: 2. Of those that a mesh axis runs over, the one named last changes fastest.
Arguments:
- dosage: bfloat16 [3072, 16384], P(('grp', 'tile'), 'mk'), parts along dimension 0, may hold values from 0 to 2
- allele_freq: float32 [32768], P(('grp', 'mk')), parts along dimension 0, may hold values from 0.05 to 0.5
- present: int32 [256, 3072], P('mk', ('grp', 'tile')), parts along dimension 1, may hold values 0 or 1
- panel_rows: int32 [32], P('grp'), parts along dimension 0, may hold values from 1 to 192, 1536 in all
Outputs:
- panels: float32 [6144, 1536], P(('grp', 'mk', 'tile')), parts along dimension 0
The draws below stay inside these ranges and needn't reach their ends.
There are 2 independent parts, one for each index of `grp`. The reference program is written for one: setup_inputs(seed, part) draws one part's arguments, and reference() takes and returns one part's arrays. A program takes and returns all parts, laid end to end along the dimension named above; each array names one. Nothing has to cross between parts.
Inputs may be any that keep to these rules, and one draw needn't show every extreme that they name: `panel_rows`: the counts sum to 1536.
All inputs are finite; a program needn't handle non-finite values. No bound on the sum of `present` on one device may be relied on, other than what follows from the above.
Results may differ from the reference program's by a relative error of at most 0.0011.
Values may be sent and summed in bfloat16 or wider, within the bound.
A program may use at most 64 MiB of HBM per device.

```python
import math
import jax
import jax.numpy as jnp
import numpy as np
from jax import lax

MB = 64
N = 1536
M = 16384
OWNERS = 16
PMAX = 192


def allele_table(key):
    return jax.random.uniform(jax.random.fold_in(key, 11), (M,), jnp.float32, 0.05, 0.5)


def draw_allele_freq(key, part):
    return allele_table(key)


def draw_dosage(key, part):
    freq = allele_table(key)
    ancestor = jax.random.randint(jax.random.fold_in(key, 13), (N,), 0, N // 2)
    shared = jax.random.uniform(jax.random.fold_in(key, 12), (N // 2, M), jnp.float32)
    first = (jnp.take(shared, ancestor, axis=0) < freq).astype(jnp.float32)
    second = (jax.random.uniform(jax.random.fold_in(key, 14), (N, M), jnp.float32) < freq).astype(jnp.float32)
    noise = 0.08 * jax.random.normal(jax.random.fold_in(key, 15), (N, M), jnp.float32)
    return jnp.clip(first + second + noise, 0.0, 2.0).astype(jnp.bfloat16)


def touch_ends(array, stream_key, least, high):
    place = [jax.random.randint(jax.random.fold_in(stream_key, axis), (), 0, length) for axis, length in enumerate(array.shape)]
    longest = array.shape.index(max(array.shape))
    neighbour = place[:longest] + [(place[longest] + 1) % array.shape[longest]] + place[longest + 1:]
    return array.at[tuple(place)].set(least).at[tuple(neighbour)].set(high)


def length_profile(amount, total, bound, skew):
    weights = [(1 << 20) // math.isqrt(grade ** skew) + 1 for grade in range(2, amount + 1)]
    surplus, counts = total - bound - (amount - 1), [1] * (amount - 1)
    while surplus > 0:
        free = [i for i in range(amount - 1) if counts[i] < bound]
        pool, remaining = sum([weights[i] for i in free]), surplus
        for i in free:
            more = min(bound - counts[i], max(1, remaining * weights[i] // pool), surplus)
            counts[i] = counts[i] + more
            surplus = surplus - more
    return np.array([bound] + counts)


def uneven(key, amount, total, bound, slope):
    if amount == 2:
        one = jax.random.randint(key, (), max(1, total - bound), min(bound, total - 1) + 1)
        return jnp.stack([one, total - one])
    lengths = jnp.asarray(length_profile(amount, total, bound, slope), jnp.int32)
    twos = (amount - 1) // 2
    giver, sink = lengths[1:1 + 2 * twos:2], lengths[2:2 + 2 * twos:2]
    margin = jnp.minimum(giver - 1, bound - sink)
    passed = jax.random.randint(jax.random.fold_in(key, 1), (twos,), 0, 1 << 20) % (margin + 1)
    lengths = lengths.at[1:1 + 2 * twos:2].set(giver - passed).at[2:2 + 2 * twos:2].set(sink + passed)
    return lengths[jax.random.permutation(jax.random.fold_in(key, 2), amount)]


def setup_inputs(seed: int = 0, part: int = 0) -> dict:
    keys = jax.random.split(jax.random.key(seed), 5)
    own_keys = jax.random.split(jax.random.fold_in(keys[4], part), 5)
    dosage = draw_dosage(jax.random.fold_in(jax.random.fold_in(keys[4], part), 71), part)
    allele_freq = draw_allele_freq(jax.random.fold_in(jax.random.fold_in(keys[4], part), 71), part)
    present = touch_ends((jax.random.randint(own_keys[2], (M // MB, N), 0, 10) < 9).astype(jnp.int32), jax.random.fold_in(own_keys[2], 1), 0, 1)
    panel_rows = uneven(own_keys[3], OWNERS, N, PMAX, 2).astype(jnp.int32)
    return {"dosage": dosage, "allele_freq": allele_freq, "present": present, "panel_rows": panel_rows}


def reference(dosage, allele_freq, present, panel_rows):
    flags = jnp.repeat(present.T, MB, axis=1).astype(jnp.float32)
    twice_freq = 2.0 * allele_freq
    scaled = (dosage.astype(jnp.float32) - twice_freq) / jnp.sqrt(twice_freq * (1.0 - allele_freq))
    standard = (flags * scaled).astype(jnp.bfloat16)
    grm = jnp.dot(standard, standard.T, preferred_element_type=jnp.float32) * (1.0 / M)
    starts = (jnp.cumsum(panel_rows) - panel_rows).astype(jnp.int32)
    padded = jnp.concatenate([grm, jnp.zeros((PMAX, N), jnp.float32)], axis=0)

    def one_panel(start, count):
        rows = lax.dynamic_slice_in_dim(padded, start, PMAX, 0)
        live = jnp.arange(PMAX) < count
        return jnp.where(live[:, None], rows, jnp.float32(0.0))
    stacked = jax.vmap(one_panel)(starts, panel_rows)
    return stacked.reshape(OWNERS * PMAX, N)
```

```python
import functools

import jax
import jax.numpy as jnp
from jax import lax
from jax.experimental import pallas as pl
from jax.experimental.pallas import tpu as pltpu
from jax.sharding import PartitionSpec as P

MESH = pl.DeviceIdType.MESH
NT = (((1,), (1,)), ((), ()))
TN = (((0,), (0,)), ((), ()))
UP = 64.0


def encode(x):
    return (x * jnp.abs(x) * (x * x)).astype(jnp.bfloat16)


def decode(v):
    v = v.astype(jnp.float32)
    root = lax.rsqrt(lax.rsqrt(jnp.abs(v)))
    return jnp.where(v == 0.0, 0.0, jnp.where(v < 0.0, -root, root))


def kernel(mk_y, mk_z, markers, dosage, freq, present, rows_ref, out, *scratch):
    half, depth = dosage.shape
    row_blk = half // 3
    hy = row_blk // mk_y
    sl = hy // mk_z
    widths = [row_blk * (a + 1) for a in range(3)] + [half // 2] * 3
    chunks = len(widths)
    it = iter(scratch)
    dos, std, hot = next(it), next(it), next(it)
    ys, yr, zs, zr, acc, fin = ([next(it) for _ in range(chunks)] for _ in range(6))
    (dos_sem, std_s, std_r, y_s, y_r, z_s, z_r, gz_s, gz_r, gy_s, gy_r, t_s, t_r) = it

    mk, t = lax.axis_index("mk"), lax.axis_index("tile")
    y, z = lax.rem(mk, mk_y), mk // mk_y
    oy, ot = 1 - y, 1 - t

    loads = [
        pltpu.make_async_copy(
            dosage.at[pl.ds(a * row_blk, row_blk)], dos.at[pl.ds(a * row_blk, row_blk)], dos_sem.at[a]
        )
        for a in range(3)
    ]
    for load in loads:
        load.start()

    to_y = {"mk": z * mk_y + oy}
    to_t = {"tile": ot}

    def to_z(k):
        return {"mk": lax.rem(z + k, mk_z) * mk_y + y}

    barrier = pltpu.get_barrier_semaphore()
    peers = [to_y, to_t] + [to_z(k) for k in range(1, mk_z)]
    for peer in peers:
        pl.semaphore_signal(barrier, inc=1, device_id=peer, device_id_type=MESH)

    owner = mk * 2 + t
    start = jnp.int32(0)
    count = jnp.int32(0)
    for k in range(rows_ref.shape[0]):
        here = rows_ref[k]
        start = start + jnp.where(k < owner, here, 0)
        count = count + jnp.where(k == owner, here, 0)
    i_row = lax.broadcasted_iota(jnp.int32, hot.shape, 0)
    i_col = lax.broadcasted_iota(jnp.int32, hot.shape, 1)
    hot[...] = jnp.where((i_col - start == i_row) & (i_row < count), 1.0, 0.0).astype(jnp.bfloat16)
    out[...] = jnp.zeros_like(out)

    flag_blocks = present.shape[0]
    per_flag = depth // flag_blocks
    twice = 2.0 * freq[...]
    scale = UP / jnp.sqrt(twice * (1.0 - freq[...]))
    COL = 512

    def standardize(a):
        def piece(p, carry):
            r0 = pl.multiple_of(a * row_blk + p * 128, 128)
            called = present[:, pl.ds(r0, 128)].astype(jnp.float32).astype(jnp.bfloat16)
            for c in range(depth // COL):
                cols = slice(c * COL, (c + 1) * COL)
                b = lax.broadcasted_iota(jnp.int32, (flag_blocks, COL), 0)
                m = lax.broadcasted_iota(jnp.int32, (flag_blocks, COL), 1) + c * COL
                spread = jnp.where((m >= b * per_flag) & (m < (b + 1) * per_flag), 1.0, 0.0).astype(jnp.bfloat16)
                flags = lax.dot_general(called, spread, TN, preferred_element_type=jnp.float32)
                scaled = (dos[pl.ds(r0, 128), cols].astype(jnp.float32) - twice[:, cols]) * scale[:, cols]
                std[pl.ds(pl.multiple_of(t * half + r0, 128), 128), cols] = (flags * scaled).astype(jnp.bfloat16)
            return carry

        lax.fori_loop(0, row_blk // 128, piece, 0)

    def place(c, core):
        a = c % 3
        if c < 3:
            return core * half + a * row_blk, core * half
        return a * row_blk, half + core * (half // 2)

    def product(c, which):
        i0, j0 = place(c, t)
        left = std[pl.ds(pl.multiple_of(i0 + which * hy, 128), hy), :]
        right = std[pl.ds(pl.multiple_of(j0, 128), widths[c]), :]
        return lax.dot_general(left, right, NT, preferred_element_type=jnp.float32)

    def remote(src, dst, send, recv, peer):
        return pltpu.make_async_remote_copy(
            src_ref=src, dst_ref=dst, send_sem=send, recv_sem=recv, device_id=peer, device_id_type=MESH
        )

    sent = []

    def go(copy):
        copy.start()
        sent.append(copy)

    def std_copy(a, core):
        view = std.at[pl.ds(pl.multiple_of(core * half + a * row_blk, 128), row_blk)]
        return remote(view, view, std_s.at[a], std_r.at[a], to_t)

    def y_copy(c):
        return remote(ys[c], yr[c], y_s.at[c], y_r.at[c], to_y)

    def zrows(r):
        return pl.ds(pl.multiple_of(r * sl, sl), sl)

    def z_copy(c, k, source):
        return remote(zs[c].at[zrows(lax.rem(z + k, mk_z))], zr[c].at[zrows(source)], z_s.at[c, k], z_r.at[c, k], to_z(k))

    def gz_copy(c, k, source):
        view = fin[c].at[t, pl.ds(pl.multiple_of(y * hy + source * sl, sl), sl)]
        return remote(view, view, gz_s.at[c, k], gz_r.at[c, k], to_z(k))

    def gy_copy(c, which):
        view = fin[c].at[t, pl.ds(pl.multiple_of(which * hy, hy), hy)]
        return remote(view, view, gy_s.at[c], gy_r.at[c], to_y)

    def t_copy(c, step, core):
        which = y if step == 0 else oy
        view = fin[c].at[core, pl.ds(pl.multiple_of(which * hy, hy), hy)]
        return remote(view, view, t_s.at[c, step], t_r.at[c, step], to_t)

    def send_half(c):
        ys[c][...] = encode(product(c, oy))
        go(y_copy(c))

    def own_half(c):
        acc[c][...] = product(c, y)

    def select(c, core):
        i0, j0 = place(c, core)
        w = widths[c]
        block = fin[c][core]
        rows = pl.ds(pl.multiple_of(i0, 128), row_blk)
        cols = pl.ds(pl.multiple_of(j0, 128), w)
        out[:, cols] += jnp.dot(hot[:, rows], block, preferred_element_type=jnp.float32)
        below = w - row_blk if c < 3 else w
        if below:
            cols = pl.ds(pl.multiple_of(j0, 128), below)
            out[:, rows] += lax.dot_general(
                hot[:, cols], block[:, :below], NT, preferred_element_type=jnp.float32
            )

    for a in range(3):
        loads[a].wait()
        standardize(a)
        if a == 0:
            pl.semaphore_wait(barrier, len(peers))
        go(std_copy(a, t))
        send_half(a)
    for a in range(3):
        own_half(a)
    for a in range(3):
        std_copy(a, ot).wait_recv()
    for a in range(3, 6):
        send_half(a)
    for a in range(3, 6):
        own_half(a)

    def stage_b(c):
        y_copy(c).wait_recv()
        total = acc[c][...] + decode(yr[c][...])
        acc[c][...] = total
        zs[c][...] = encode(total)
        for k in range(1, mk_z):
            go(z_copy(c, k, z))

    def stage_c(c):
        total = acc[c][zrows(z), :]
        for k in range(1, mk_z):
            source = lax.rem(z + mk_z - k, mk_z)
            z_copy(c, k, source).wait_recv()
            total = total + decode(zr[c][zrows(source), :])
        fin[c][t, pl.ds(pl.multiple_of(y * hy + z * sl, sl), sl), :] = encode(total)
        for k in range(1, mk_z):
            go(gz_copy(c, k, z))

    def stage_d(c):
        for k in range(1, mk_z):
            gz_copy(c, k, lax.rem(z + mk_z - k, mk_z)).wait_recv()
        go(gy_copy(c, y))
        go(t_copy(c, 0, t))

    def stage_e(c):
        gy_copy(c, oy).wait_recv()
        go(t_copy(c, 1, t))
        select(c, t)

    def stage_f(c):
        t_copy(c, 0, ot).wait_recv()
        t_copy(c, 1, ot).wait_recv()
        select(c, ot)

    stages = [stage_b, stage_c, stage_d, stage_e, stage_f]
    for s in range(chunks + len(stages) - 1):
        for d, stage in enumerate(stages):
            if 0 <= s - d < chunks:
                stage(s - d)
    for r in range(0, out.shape[0], 32):
        out[r : r + 32, :] = decode(out[r : r + 32, :]) * (1.0 / (markers * UP * UP))
    for copy in sent:
        copy.wait_send()


def fused(mesh, dosage, allele_freq, present, panel_rows):
    mk_y, mk_z = 2, mesh.shape["mk"] // 2
    half, depth = dosage.shape
    samples = 2 * half
    panel_max = 2 * samples // (2 * mesh.shape["mk"])
    row_blk = half // 3
    widths = [row_blk * (a + 1) for a in range(3)] + [half // 2] * 3
    hy = row_blk // 2
    bf, f32 = jnp.bfloat16, jnp.float32
    scratch = [pltpu.VMEM((half, depth), bf), pltpu.VMEM((samples, depth), bf), pltpu.VMEM((panel_max, samples), bf)]
    for dtype in (bf, bf, bf, bf, f32):
        scratch += [pltpu.VMEM((hy, w), dtype) for w in widths]
    scratch += [pltpu.VMEM((2, row_blk, w), bf) for w in widths]
    n = len(widths)
    for shape in [(3,)] * 3 + [(n,)] * 2 + [(n, mk_z)] * 4 + [(n,)] * 2 + [(n, 2)] * 2:
        scratch.append(pltpu.SemaphoreType.DMA(shape))
    vmem = pl.BlockSpec(memory_space=pltpu.VMEM)
    return pl.pallas_call(
        functools.partial(kernel, mk_y, mk_z, depth * mesh.shape["mk"]),
        out_shape=jax.ShapeDtypeStruct((panel_max, samples), f32),
        in_specs=[pl.BlockSpec(memory_space=pl.ANY), vmem, vmem, pl.BlockSpec(memory_space=pltpu.SMEM)],
        out_specs=vmem,
        scratch_shapes=scratch,
        compiler_params=pltpu.CompilerParams(
            collective_id=0, has_side_effects=True, vmem_limit_bytes=44 * 1024 * 1024
        ),
    )(dosage, allele_freq.reshape(1, depth), present, panel_rows)


def general(dosage, allele_freq, present, panel_rows):
    tile_count = lax.axis_size("tile")
    local_markers = dosage.shape[1]
    marker_total = local_markers * lax.axis_size("mk")
    flags = jnp.repeat(present.T, local_markers // present.shape[0], axis=1).astype(jnp.float32)
    twice_freq = 2.0 * allele_freq
    scaled = (dosage.astype(jnp.float32) - twice_freq) / jnp.sqrt(twice_freq * (1.0 - allele_freq))
    standard = (flags * scaled).astype(jnp.bfloat16)
    all_rows = lax.all_gather(standard, "tile", axis=0, tiled=True)
    samples = all_rows.shape[0]
    owner_count = lax.axis_size("mk") * tile_count
    panel_max = 2 * samples // owner_count
    order = jnp.arange(owner_count)
    starts = jnp.sum(jnp.where(order[None, :] < order[:, None], panel_rows[None, :], 0), axis=1)
    row_ids = jnp.arange(panel_max * tile_count * lax.axis_size("mk"), dtype=jnp.int32)
    owner_ids = row_ids // panel_max
    within = row_ids - owner_ids * panel_max
    sample_ids = jnp.take(starts, owner_ids) + within
    live = within < jnp.take(panel_rows, owner_ids)
    picked = jnp.take(all_rows, jnp.clip(sample_ids, 0, samples - 1), axis=0)
    picked = jnp.where(live[:, None], picked, jnp.zeros((), jnp.bfloat16))
    product = jnp.einsum("rm,sm->rs", picked, standard, preferred_element_type=jnp.float32)
    pair_rows = lax.psum_scatter(
        product * (1.0 / marker_total), "mk", scatter_dimension=0, tiled=True
    )
    return lax.all_to_all(pair_rows, "tile", split_axis=0, concat_axis=1, tiled=True)


def solution(mesh):
    in_specs = (P(("grp", "tile"), "mk"), P(("grp", "mk")), P("mk", ("grp", "tile")), P("grp"))
    out_specs = P(("grp", "mk", "tile"), None)
    local = functools.partial(fused, mesh) if mesh.shape["mk"] == 8 else general
    return jax.shard_map(local, mesh=mesh, in_specs=in_specs, out_specs=out_specs, check_vma=False)
```

```python
import functools

import jax
import jax.numpy as jnp
from jax import lax
from jax.experimental import pallas as pl
from jax.experimental.pallas import tpu as pltpu
from jax.sharding import PartitionSpec as P

MESH = pl.DeviceIdType.MESH
NT = (((1,), (1,)), ((), ()))
TN = (((0,), (0,)), ((), ()))
UP = 64.0


def encode(x):
    return (x * jnp.abs(x) * (x * x)).astype(jnp.bfloat16)


def decode(v):
    v = v.astype(jnp.float32)
    root = lax.rsqrt(lax.rsqrt(jnp.abs(v)))
    return jnp.where(v == 0.0, 0.0, jnp.where(v < 0.0, -root, root))


Y_FIRST, Z_FIRST = (0, 1, 2), (1, 0, 2)
ORDERS = [Y_FIRST] * 6


def kernel(markers, dosage, freq_hbm, present_hbm, rows_hbm, out, *scratch):
    half, depth = dosage.shape
    row_blk = half // 3
    size = [row_blk // 2, row_blk // 4, row_blk // 8]
    hy = size[0]
    widths = [row_blk * (a + 1) for a in range(3)] + [half // 2] * 3
    chunks = len(widths)
    it = iter(scratch)
    dos, std, hot, freq, present, rows_ref = (next(it) for _ in range(6))
    out_buf = [[next(it) for _ in range(chunks)] for _ in range(3)]
    in_buf = [[next(it) for _ in range(chunks)] for _ in range(3)]
    acc, fin = ([next(it) for _ in range(chunks)] for _ in range(2))
    (load_sem, std_s, std_r, red_s, red_r, gat_s, gat_r, t_s, t_r) = it

    mk, t = lax.axis_index("mk"), lax.axis_index("tile")
    y, z = lax.rem(mk, 2), mk // 2
    low, high = lax.rem(z, 2), z // 2
    bits = [y, low, high]
    partners = [{"mk": mk + 1 - 2 * y}, {"mk": mk + 2 - 4 * low}, {"mk": mk + 4 - 8 * high}]
    ot = 1 - t
    to_t = {"tile": ot}

    loads = [
        pltpu.make_async_copy(present_hbm, present, load_sem.at[3]),
        pltpu.make_async_copy(freq_hbm, freq, load_sem.at[4]),
        pltpu.make_async_copy(rows_hbm, rows_ref, load_sem.at[5]),
    ]
    for load in loads:
        load.start()
    dos_loads = [
        pltpu.make_async_copy(
            dosage.at[pl.ds(a * row_blk, row_blk)], dos.at[pl.ds(a * row_blk, row_blk)], load_sem.at[a]
        )
        for a in range(3)
    ]
    for load in dos_loads:
        load.start()

    barrier = pltpu.get_barrier_semaphore()
    peers = partners + [to_t]
    for peer in peers:
        pl.semaphore_signal(barrier, inc=1, device_id=peer, device_id_type=MESH)
    for load in loads:
        load.wait()

    owner = mk * 2 + t
    start = jnp.int32(0)
    count = jnp.int32(0)
    for k in range(rows_ref.shape[0]):
        here = rows_ref[k]
        start = start + jnp.where(k < owner, here, 0)
        count = count + jnp.where(k == owner, here, 0)
    i_row = lax.broadcasted_iota(jnp.int32, hot.shape, 0)
    i_col = lax.broadcasted_iota(jnp.int32, hot.shape, 1)
    hot[...] = jnp.where((i_col - start == i_row) & (i_row < count), 1.0, 0.0).astype(jnp.bfloat16)
    out[...] = jnp.zeros_like(out)

    flag_blocks = present.shape[0]
    per_flag = depth // flag_blocks
    twice = 2.0 * freq[...]
    scale = UP / jnp.sqrt(twice * (1.0 - freq[...]))
    COL = 512

    def standardize(a):
        def piece(p, carry):
            r0 = pl.multiple_of(a * row_blk + p * 128, 128)
            called = present[:, pl.ds(r0, 128)].astype(jnp.float32).astype(jnp.bfloat16)
            for c in range(depth // COL):
                cols = slice(c * COL, (c + 1) * COL)
                b = lax.broadcasted_iota(jnp.int32, (flag_blocks, COL), 0)
                m = lax.broadcasted_iota(jnp.int32, (flag_blocks, COL), 1) + c * COL
                spread = jnp.where((m >= b * per_flag) & (m < (b + 1) * per_flag), 1.0, 0.0).astype(jnp.bfloat16)
                flags = lax.dot_general(called, spread, TN, preferred_element_type=jnp.float32)
                scaled = (dos[pl.ds(r0, 128), cols].astype(jnp.float32) - twice[:, cols]) * scale[:, cols]
                std[pl.ds(pl.multiple_of(t * half + r0, 128), 128), cols] = (flags * scaled).astype(jnp.bfloat16)
            return carry

        lax.fori_loop(0, row_blk // 128, piece, 0)

    def place(c, core):
        a = c % 3
        if c < 3:
            return core * half + a * row_blk, core * half
        return a * row_blk, half + core * (half // 2)

    def product(c, which):
        i0, j0 = place(c, t)
        left = std[pl.ds(pl.multiple_of(i0 + which * hy, 128), hy), :]
        right = std[pl.ds(pl.multiple_of(j0, 128), widths[c]), :]
        return lax.dot_general(left, right, NT, preferred_element_type=jnp.float32)

    def remote(src, dst, send, recv, peer):
        return pltpu.make_async_remote_copy(
            src_ref=src, dst_ref=dst, send_sem=send, recv_sem=recv, device_id=peer, device_id_type=MESH
        )

    sent = []

    def go(copy):
        copy.start()
        sent.append(copy)

    def std_copy(a, core):
        view = std.at[pl.ds(pl.multiple_of(core * half + a * row_blk, 128), row_blk)]
        return remote(view, view, std_s.at[a], std_r.at[a], to_t)

    def base(c, level):
        row = 0
        for l in range(level):
            row = row + bits[ORDERS[c][l]] * size[l]
        return row

    def red_copy(c, l):
        return remote(out_buf[l][c], in_buf[l][c], red_s.at[c, l], red_r.at[c, l], partners[ORDERS[c][l]])

    def gat_copy(c, l, mine):
        bit = bits[ORDERS[c][l]]
        row = base(c, l) + (bit if mine else 1 - bit) * size[l]
        view = fin[c].at[t, pl.ds(pl.multiple_of(row, size[l]), size[l])]
        return remote(view, view, gat_s.at[c, l], gat_r.at[c, l], partners[ORDERS[c][l]])

    def t_copy(c, step, core):
        bit = bits[ORDERS[c][0]]
        which = bit if step == 0 else 1 - bit
        view = fin[c].at[core, pl.ds(pl.multiple_of(which * hy, hy), hy)]
        return remote(view, view, t_s.at[c, step], t_r.at[c, step], to_t)

    def send_half(c):
        out_buf[0][c][...] = encode(product(c, 1 - bits[ORDERS[c][0]]))
        go(red_copy(c, 0))

    def own_half(c):
        acc[c][...] = product(c, bits[ORDERS[c][0]])

    def select(c, core):
        i0, j0 = place(c, core)
        w = widths[c]
        block = fin[c][core]
        rows = pl.ds(pl.multiple_of(i0, 128), row_blk)
        cols = pl.ds(pl.multiple_of(j0, 128), w)
        out[:, cols] += jnp.dot(hot[:, rows], block, preferred_element_type=jnp.float32)
        below = w - row_blk if c < 3 else w
        if below:
            cols = pl.ds(pl.multiple_of(j0, 128), below)
            out[:, rows] += lax.dot_general(
                hot[:, cols], block[:, :below], NT, preferred_element_type=jnp.float32
            )

    for a in range(3):
        dos_loads[a].wait()
        standardize(a)
        if a == 0:
            pl.semaphore_wait(barrier, len(peers))
        go(std_copy(a, t))
        send_half(a)
    for a in range(3):
        own_half(a)
    for a in range(3):
        std_copy(a, ot).wait_recv()
    for a in range(3, 6):
        send_half(a)
    for a in range(3, 6):
        own_half(a)

    def halve(c, l):
        red_copy(c, l - 1).wait_recv()
        rows = pl.ds(0, size[l - 1])
        acc[c][rows, :] = acc[c][rows, :] + decode(in_buf[l - 1][c][...])
        bit = bits[ORDERS[c][l]]
        other = pl.ds(pl.multiple_of((1 - bit) * size[l], size[l]), size[l])
        mine = pl.ds(pl.multiple_of(bit * size[l], size[l]), size[l])
        out_buf[l][c][...] = encode(acc[c][other, :])
        go(red_copy(c, l))
        acc[c][pl.ds(0, size[l]), :] = acc[c][mine, :]

    def finish(c):
        red_copy(c, 2).wait_recv()
        total = acc[c][pl.ds(0, size[2]), :] + decode(in_buf[2][c][...])
        fin[c][t, pl.ds(pl.multiple_of(base(c, 3), size[2]), size[2]), :] = encode(total)
        go(gat_copy(c, 2, True))

    def gather_1(c):
        gat_copy(c, 2, False).wait_recv()
        go(gat_copy(c, 1, True))

    def gather_2(c):
        gat_copy(c, 1, False).wait_recv()
        go(gat_copy(c, 0, True))
        go(t_copy(c, 0, t))

    def gather_3(c):
        gat_copy(c, 0, False).wait_recv()
        go(t_copy(c, 1, t))
        select(c, t)

    def others(c):
        t_copy(c, 0, ot).wait_recv()
        t_copy(c, 1, ot).wait_recv()
        select(c, ot)

    stages = [
        functools.partial(halve, l=1), functools.partial(halve, l=2),
        finish, gather_1, gather_2, gather_3, others,
    ]
    for s in range(chunks + len(stages) - 1):
        for d, stage in enumerate(stages):
            if 0 <= s - d < chunks:
                stage(s - d)
    for r in range(0, out.shape[0], 32):
        out[r : r + 32, :] = decode(out[r : r + 32, :]) * (1.0 / (markers * UP * UP))
    for copy in sent:
        copy.wait_send()


def fused(mesh, dosage, allele_freq, present, panel_rows):
    half, depth = dosage.shape
    samples = 2 * half
    panel_max = 2 * samples // (2 * mesh.shape["mk"])
    row_blk = half // 3
    widths = [row_blk * (a + 1) for a in range(3)] + [half // 2] * 3
    bf, f32 = jnp.bfloat16, jnp.float32
    scratch = [
        pltpu.VMEM((half, depth), bf), pltpu.VMEM((samples, depth), bf), pltpu.VMEM((panel_max, samples), bf),
        pltpu.VMEM((1, depth), f32), pltpu.VMEM(present.shape, present.dtype),
        pltpu.SMEM(panel_rows.shape, panel_rows.dtype),
    ]
    for _ in range(2):
        for parts in (2, 4, 8):
            scratch += [pltpu.VMEM((row_blk // parts, w), bf) for w in widths]
    scratch += [pltpu.VMEM((row_blk // 2, w), f32) for w in widths]
    scratch += [pltpu.VMEM((2, row_blk, w), bf) for w in widths]
    n = len(widths)
    for shape in [(6,)] + [(3,)] * 2 + [(n, 3)] * 4 + [(n, 2)] * 2:
        scratch.append(pltpu.SemaphoreType.DMA(shape))
    return pl.pallas_call(
        functools.partial(kernel, depth * mesh.shape["mk"]),
        out_shape=jax.ShapeDtypeStruct((panel_max, samples), f32),
        in_specs=[pl.BlockSpec(memory_space=pltpu.HBM)] * 4,
        out_specs=pl.BlockSpec(memory_space=pltpu.VMEM),
        scratch_shapes=scratch,
        compiler_params=pltpu.CompilerParams(
            collective_id=0, has_side_effects=True, vmem_limit_bytes=44 * 1024 * 1024
        ),
    )(dosage, allele_freq.reshape(1, depth), present, panel_rows)


def general(dosage, allele_freq, present, panel_rows):
    tile_count = lax.axis_size("tile")
    local_markers = dosage.shape[1]
    marker_total = local_markers * lax.axis_size("mk")
    flags = jnp.repeat(present.T, local_markers // present.shape[0], axis=1).astype(jnp.float32)
    twice_freq = 2.0 * allele_freq
    scaled = (dosage.astype(jnp.float32) - twice_freq) / jnp.sqrt(twice_freq * (1.0 - allele_freq))
    standard = (flags * scaled).astype(jnp.bfloat16)
    all_rows = lax.all_gather(standard, "tile", axis=0, tiled=True)
    samples = all_rows.shape[0]
    owner_count = lax.axis_size("mk") * tile_count
    panel_max = 2 * samples // owner_count
    order = jnp.arange(owner_count)
    starts = jnp.sum(jnp.where(order[None, :] < order[:, None], panel_rows[None, :], 0), axis=1)
    row_ids = jnp.arange(panel_max * tile_count * lax.axis_size("mk"), dtype=jnp.int32)
    owner_ids = row_ids // panel_max
    within = row_ids - owner_ids * panel_max
    sample_ids = jnp.take(starts, owner_ids) + within
    live = within < jnp.take(panel_rows, owner_ids)
    picked = jnp.take(all_rows, jnp.clip(sample_ids, 0, samples - 1), axis=0)
    picked = jnp.where(live[:, None], picked, jnp.zeros((), jnp.bfloat16))
    product = jnp.einsum("rm,sm->rs", picked, standard, preferred_element_type=jnp.float32)
    pair_rows = lax.psum_scatter(
        product * (1.0 / marker_total), "mk", scatter_dimension=0, tiled=True
    )
    return lax.all_to_all(pair_rows, "tile", split_axis=0, concat_axis=1, tiled=True)


def solution(mesh):
    in_specs = (P(("grp", "tile"), "mk"), P(("grp", "mk")), P("mk", ("grp", "tile")), P("grp"))
    out_specs = P(("grp", "mk", "tile"), None)
    local = functools.partial(fused, mesh) if mesh.shape["mk"] == 8 else general
    return jax.shard_map(local, mesh=mesh, in_specs=in_specs, out_specs=out_specs, check_vma=False)
```

```python
import functools

import jax
import jax.numpy as jnp
from jax import lax
from jax.experimental import pallas as pl
from jax.experimental.pallas import tpu as pltpu
from jax.sharding import PartitionSpec as P

MESH = pl.DeviceIdType.MESH
NT = (((1,), (1,)), ((), ()))
TN = (((0,), (0,)), ((), ()))
UP = 64.0


def encode(x):
    return (x * jnp.abs(x) * (x * x)).astype(jnp.bfloat16)


def decode(v):
    v = v.astype(jnp.float32)
    root = lax.rsqrt(lax.rsqrt(jnp.abs(v)))
    return jnp.where(v == 0.0, 0.0, jnp.where(v < 0.0, -root, root))


Y_FIRST, Z_FIRST = (0, 1, 2), (1, 0, 2)
ORDERS = [Y_FIRST] * 6
AHEAD = 2


def kernel(markers, dosage, freq_hbm, present_hbm, rows_hbm, out, *scratch):
    half, depth = dosage.shape
    row_blk = half // 3
    size = [row_blk // 2, row_blk // 4, row_blk // 8]
    hy = size[0]
    widths = [row_blk * (a + 1) for a in range(3)] + [half // 2] * 3
    chunks = len(widths)
    it = iter(scratch)
    dos, std, hot, freq, present, rows_ref = (next(it) for _ in range(6))
    out_buf = [[next(it) for _ in range(chunks)] for _ in range(3)]
    in_buf = [[next(it) for _ in range(chunks)] for _ in range(3)]
    acc, fin = ([next(it) for _ in range(chunks)] for _ in range(2))
    (load_sem, std_s, std_r, red_s, red_r, gat_s, gat_r, t_s, t_r) = it

    mk, t = lax.axis_index("mk"), lax.axis_index("tile")
    y, z = lax.rem(mk, 2), mk // 2
    low, high = lax.rem(z, 2), z // 2
    bits = [y, low, high]
    partners = [{"mk": mk + 1 - 2 * y}, {"mk": mk + 2 - 4 * low}, {"mk": mk + 4 - 8 * high}]
    ot = 1 - t
    to_t = {"tile": ot}

    loads = [
        pltpu.make_async_copy(present_hbm, present, load_sem.at[3]),
        pltpu.make_async_copy(freq_hbm, freq, load_sem.at[4]),
        pltpu.make_async_copy(rows_hbm, rows_ref, load_sem.at[5]),
    ]
    for load in loads:
        load.start()
    dos_loads = [
        pltpu.make_async_copy(
            dosage.at[pl.ds(a * row_blk, row_blk)], dos.at[pl.ds(a * row_blk, row_blk)], load_sem.at[a]
        )
        for a in range(3)
    ]
    for load in dos_loads:
        load.start()

    barrier = pltpu.get_barrier_semaphore()
    peers = partners + [to_t]
    for peer in peers:
        pl.semaphore_signal(barrier, inc=1, device_id=peer, device_id_type=MESH)
    for load in loads:
        load.wait()

    owner = mk * 2 + t
    start = jnp.int32(0)
    count = jnp.int32(0)
    for k in range(rows_ref.shape[0]):
        here = rows_ref[k]
        start = start + jnp.where(k < owner, here, 0)
        count = count + jnp.where(k == owner, here, 0)
    i_row = lax.broadcasted_iota(jnp.int32, hot.shape, 0)
    i_col = lax.broadcasted_iota(jnp.int32, hot.shape, 1)
    hot[...] = jnp.where((i_col - start == i_row) & (i_row < count), 1.0, 0.0).astype(jnp.bfloat16)
    out[...] = jnp.zeros_like(out)

    flag_blocks = present.shape[0]
    per_flag = depth // flag_blocks
    twice = 2.0 * freq[...]
    scale = UP / jnp.sqrt(twice * (1.0 - freq[...]))
    COL = 512

    def standardize(a):
        def piece(p, carry):
            r0 = pl.multiple_of(a * row_blk + p * 128, 128)
            called = present[:, pl.ds(r0, 128)].astype(jnp.float32).astype(jnp.bfloat16)
            for c in range(depth // COL):
                cols = slice(c * COL, (c + 1) * COL)
                b = lax.broadcasted_iota(jnp.int32, (flag_blocks, COL), 0)
                m = lax.broadcasted_iota(jnp.int32, (flag_blocks, COL), 1) + c * COL
                spread = jnp.where((m >= b * per_flag) & (m < (b + 1) * per_flag), 1.0, 0.0).astype(jnp.bfloat16)
                flags = lax.dot_general(called, spread, TN, preferred_element_type=jnp.float32)
                scaled = (dos[pl.ds(r0, 128), cols].astype(jnp.float32) - twice[:, cols]) * scale[:, cols]
                std[pl.ds(pl.multiple_of(t * half + r0, 128), 128), cols] = (flags * scaled).astype(jnp.bfloat16)
            return carry

        lax.fori_loop(0, row_blk // 128, piece, 0)

    def place(c, core):
        a = c % 3
        if c < 3:
            return core * half + a * row_blk, core * half
        return a * row_blk, half + core * (half // 2)

    def product(c, which):
        i0, j0 = place(c, t)
        left = std[pl.ds(pl.multiple_of(i0 + which * hy, 128), hy), :]
        right = std[pl.ds(pl.multiple_of(j0, 128), widths[c]), :]
        return lax.dot_general(left, right, NT, preferred_element_type=jnp.float32)

    def remote(src, dst, send, recv, peer):
        return pltpu.make_async_remote_copy(
            src_ref=src, dst_ref=dst, send_sem=send, recv_sem=recv, device_id=peer, device_id_type=MESH
        )

    sent = []

    def go(copy):
        copy.start()
        sent.append(copy)

    def std_copy(a, core):
        view = std.at[pl.ds(pl.multiple_of(core * half + a * row_blk, 128), row_blk)]
        return remote(view, view, std_s.at[a], std_r.at[a], to_t)

    def base(c, level):
        row = 0
        for l in range(level):
            row = row + bits[ORDERS[c][l]] * size[l]
        return row

    def red_copy(c, l):
        return remote(out_buf[l][c], in_buf[l][c], red_s.at[c, l], red_r.at[c, l], partners[ORDERS[c][l]])

    def gat_copy(c, l, mine):
        bit = bits[ORDERS[c][l]]
        row = base(c, l) + (bit if mine else 1 - bit) * size[l]
        view = fin[c].at[t, pl.ds(pl.multiple_of(row, size[l]), size[l])]
        return remote(view, view, gat_s.at[c, l], gat_r.at[c, l], partners[ORDERS[c][l]])

    def t_copy(c, step, core):
        bit = bits[ORDERS[c][0]]
        which = bit if step == 0 else 1 - bit
        view = fin[c].at[core, pl.ds(pl.multiple_of(which * hy, hy), hy)]
        return remote(view, view, t_s.at[c, step], t_r.at[c, step], to_t)

    first = []

    def send_half(c):
        out_buf[0][c][...] = encode(product(c, 1 - bits[ORDERS[c][0]]))
        if c >= AHEAD:
            first[c - AHEAD].wait_send()
        first.append(red_copy(c, 0))
        first[c].start()

    def own_half(c):
        acc[c][...] = product(c, bits[ORDERS[c][0]])

    def select(c, core):
        i0, j0 = place(c, core)
        w = widths[c]
        block = fin[c][core]
        rows = pl.ds(pl.multiple_of(i0, 128), row_blk)
        cols = pl.ds(pl.multiple_of(j0, 128), w)
        out[:, cols] += jnp.dot(hot[:, rows], block, preferred_element_type=jnp.float32)
        below = w - row_blk if c < 3 else w
        if below:
            cols = pl.ds(pl.multiple_of(j0, 128), below)
            out[:, rows] += lax.dot_general(
                hot[:, cols], block[:, :below], NT, preferred_element_type=jnp.float32
            )

    for a in range(3):
        dos_loads[a].wait()
        standardize(a)
        if a == 0:
            pl.semaphore_wait(barrier, len(peers))
        go(std_copy(a, t))
        send_half(a)
    def halve(c, l):
        red_copy(c, l - 1).wait_recv()
        rows = pl.ds(0, size[l - 1])
        acc[c][rows, :] = acc[c][rows, :] + decode(in_buf[l - 1][c][...])
        bit = bits[ORDERS[c][l]]
        other = pl.ds(pl.multiple_of((1 - bit) * size[l], size[l]), size[l])
        mine = pl.ds(pl.multiple_of(bit * size[l], size[l]), size[l])
        out_buf[l][c][...] = encode(acc[c][other, :])
        go(red_copy(c, l))
        acc[c][pl.ds(0, size[l]), :] = acc[c][mine, :]

    def finish(c):
        red_copy(c, 2).wait_recv()
        total = acc[c][pl.ds(0, size[2]), :] + decode(in_buf[2][c][...])
        fin[c][t, pl.ds(pl.multiple_of(base(c, 3), size[2]), size[2]), :] = encode(total)
        go(gat_copy(c, 2, True))

    def gather_1(c):
        gat_copy(c, 2, False).wait_recv()
        go(gat_copy(c, 1, True))

    def gather_2(c):
        gat_copy(c, 1, False).wait_recv()
        go(gat_copy(c, 0, True))
        go(t_copy(c, 0, t))

    def gather_3(c):
        gat_copy(c, 0, False).wait_recv()
        go(t_copy(c, 1, t))
        select(c, t)

    def others(c):
        t_copy(c, 0, ot).wait_recv()
        t_copy(c, 1, ot).wait_recv()
        select(c, ot)

    stages = [
        functools.partial(halve, l=1), functools.partial(halve, l=2),
        finish, gather_1, gather_2, gather_3, others,
    ]
    for a in range(3):
        own_half(a)
    for s in range(chunks + len(stages) - 1):
        if s == 1:
            for a in range(3):
                std_copy(a, ot).wait_recv()
        if 1 <= s <= 3:
            send_half(s + 2)
            own_half(s + 2)
        for d, stage in enumerate(stages):
            if 0 <= s - d < chunks:
                stage(s - d)
    for r in range(0, out.shape[0], 32):
        out[r : r + 32, :] = decode(out[r : r + 32, :]) * (1.0 / (markers * UP * UP))
    for copy in sent + first[chunks - AHEAD :]:
        copy.wait_send()


def fused(mesh, dosage, allele_freq, present, panel_rows):
    half, depth = dosage.shape
    samples = 2 * half
    panel_max = 2 * samples // (2 * mesh.shape["mk"])
    row_blk = half // 3
    widths = [row_blk * (a + 1) for a in range(3)] + [half // 2] * 3
    bf, f32 = jnp.bfloat16, jnp.float32
    scratch = [
        pltpu.VMEM((half, depth), bf), pltpu.VMEM((samples, depth), bf), pltpu.VMEM((panel_max, samples), bf),
        pltpu.VMEM((1, depth), f32), pltpu.VMEM(present.shape, present.dtype),
        pltpu.SMEM(panel_rows.shape, panel_rows.dtype),
    ]
    for _ in range(2):
        for parts in (2, 4, 8):
            scratch += [pltpu.VMEM((row_blk // parts, w), bf) for w in widths]
    scratch += [pltpu.VMEM((row_blk // 2, w), f32) for w in widths]
    scratch += [pltpu.VMEM((2, row_blk, w), bf) for w in widths]
    n = len(widths)
    for shape in [(6,)] + [(3,)] * 2 + [(n, 3)] * 4 + [(n, 2)] * 2:
        scratch.append(pltpu.SemaphoreType.DMA(shape))
    return pl.pallas_call(
        functools.partial(kernel, depth * mesh.shape["mk"]),
        out_shape=jax.ShapeDtypeStruct((panel_max, samples), f32),
        in_specs=[pl.BlockSpec(memory_space=pltpu.HBM)] * 4,
        out_specs=pl.BlockSpec(memory_space=pltpu.VMEM),
        scratch_shapes=scratch,
        compiler_params=pltpu.CompilerParams(
            collective_id=0, has_side_effects=True, vmem_limit_bytes=44 * 1024 * 1024
        ),
    )(dosage, allele_freq.reshape(1, depth), present, panel_rows)


def general(dosage, allele_freq, present, panel_rows):
    tile_count = lax.axis_size("tile")
    local_markers = dosage.shape[1]
    marker_total = local_markers * lax.axis_size("mk")
    flags = jnp.repeat(present.T, local_markers // present.shape[0], axis=1).astype(jnp.float32)
    twice_freq = 2.0 * allele_freq
    scaled = (dosage.astype(jnp.float32) - twice_freq) / jnp.sqrt(twice_freq * (1.0 - allele_freq))
    standard = (flags * scaled).astype(jnp.bfloat16)
    all_rows = lax.all_gather(standard, "tile", axis=0, tiled=True)
    samples = all_rows.shape[0]
    owner_count = lax.axis_size("mk") * tile_count
    panel_max = 2 * samples // owner_count
    order = jnp.arange(owner_count)
    starts = jnp.sum(jnp.where(order[None, :] < order[:, None], panel_rows[None, :], 0), axis=1)
    row_ids = jnp.arange(panel_max * tile_count * lax.axis_size("mk"), dtype=jnp.int32)
    owner_ids = row_ids // panel_max
    within = row_ids - owner_ids * panel_max
    sample_ids = jnp.take(starts, owner_ids) + within
    live = within < jnp.take(panel_rows, owner_ids)
    picked = jnp.take(all_rows, jnp.clip(sample_ids, 0, samples - 1), axis=0)
    picked = jnp.where(live[:, None], picked, jnp.zeros((), jnp.bfloat16))
    product = jnp.einsum("rm,sm->rs", picked, standard, preferred_element_type=jnp.float32)
    pair_rows = lax.psum_scatter(
        product * (1.0 / marker_total), "mk", scatter_dimension=0, tiled=True
    )
    return lax.all_to_all(pair_rows, "tile", split_axis=0, concat_axis=1, tiled=True)


def solution(mesh):
    in_specs = (P(("grp", "tile"), "mk"), P(("grp", "mk")), P("mk", ("grp", "tile")), P("grp"))
    out_specs = P(("grp", "mk", "tile"), None)
    local = functools.partial(fused, mesh) if mesh.shape["mk"] == 8 else general
    return jax.shard_map(local, mesh=mesh, in_specs=in_specs, out_specs=out_specs, check_vma=False)
```
